256 devices in a mesh: segment: 4 (over y_lo, core), tp: 64 (over x, y_hi, z).
Axes of the slice: x: 4, y: 4 (y_hi: 2, y_lo: 2; y = y_hi * 2 + y_lo), z: 8, core: 2. Of those that a mesh axis runs over, the one named last changes fastest.
Arguments:
- top_grad: bfloat16 [2, 128, 4096], P(None, None, 'tp'), may hold values from -6 to 6
- saved_in: bfloat16 [2, 4, 128, 4096], P(None, 'segment', None, 'tp'), may hold values from -6 to 6
- saved_pre: bfloat16 [2, 4, 128, 16384], P(None, 'segment', None, 'tp'), may hold values from -6 to 6
- w_up: bfloat16 [2, 4, 4096, 16384], P(None, 'segment', None, 'tp'), as said below
- w_down: bfloat16 [2, 4, 16384, 4096], P(None, 'segment', 'tp'), as said below
- mask_up: int32 [2, 4, 32, 128], P(None, 'segment', None, 'tp'), may hold values from 0 to 1, as said below
- mask_down: int32 [2, 4, 128, 32], P(None, 'segment', 'tp'), may hold values from 0 to 1, as said below
Outputs:
- all_grads: bfloat16 [2, 4, 128, 4096], P(None, 'segment', None, 'tp')
- grad_up: bfloat16 [2, 4, 2048, 16384], P(None, 'segment', None, 'tp')
- grad_down: bfloat16 [2, 4, 16384, 2048], P(None, 'segment', 'tp')
The draws below stay inside these ranges and needn't reach their ends.
Inputs may be any that keep to these rules, and one draw needn't show every extreme that they name: `mask_up`: 0 or 1; in every row, of each aligned pair of blocks along the hidden units (blocks 2j and 2j + 1) exactly one is 1; entry [1, s] equals entry [0, 3 - s]. `mask_down`: 0 or 1; in every column, of each aligned pair of blocks along the hidden units (blocks 2j and 2j + 1) exactly one is 1; entry [1, s] equals entry [0, 3 - s]. `w_up`: entry [1, s] equals entry [0, 3 - s]. `w_down`: entry [1, s] equals entry [0, 3 - s].
All inputs are finite; a program needn't handle non-finite values.
Results may differ from the reference program's by a relative error of at most 0.017.
Values may be sent and summed in bfloat16 or wider, within the bound.
No kernel may reach another device: no remote copies, remote signals or barrier semaphores. Data moves between devices by JAX's collectives and lax.ppermute only.
A program may use at most 128 MiB of HBM per device.

```python
import math
import jax
import jax.numpy as jnp

D = 4096
FF = 16384
BLOCK = 128
TOK = 128
SEGMENTS = 4
DB = 32
FB = 128


def mirrored(base):
    return jnp.stack([base, base[::-1]])


def weight_base(key, rows, cols, scale):
    return jax.random.truncated_normal(key, -3.0, 3.0, (SEGMENTS, rows, cols), jnp.float32) * scale


def draw_w_up(key, part):
    key = jax.random.fold_in(key, 11)
    return mirrored(weight_base(key, D, FF, 2.0 / math.sqrt(D))).astype(jnp.bfloat16)


def draw_w_down(key, part):
    key = jax.random.fold_in(key, 23)
    return mirrored(weight_base(key, FF, D, 2.0 / math.sqrt(FF))).astype(jnp.bfloat16)


def draw_mask_up(key, part):
    key = jax.random.fold_in(key, 37)
    picks = jax.random.randint(key, (SEGMENTS, DB, FB // 2), 0, 2, jnp.int32)
    paired = jnp.stack([1 - picks, picks], axis=-1).reshape(SEGMENTS, DB, FB)
    return mirrored(paired)


def draw_mask_down(key, part):
    key = jax.random.fold_in(key, 41)
    picks = jax.random.randint(key, (SEGMENTS, FB // 2, DB), 0, 2, jnp.int32)
    paired = jnp.stack([1 - picks, picks], axis=2).reshape(SEGMENTS, FB, DB)
    return mirrored(paired)


def shard_levels(rng, shape, split, smallest, largest):
    def one(position, shards_of):
        heights = jax.random.uniform(jax.random.fold_in(jax.random.fold_in(rng, 6), position), (shards_of,), jnp.float32, smallest / len(split), largest / len(split))
        return jnp.repeat(jnp.exp(heights), shape[position] // shards_of).reshape((-1,) + (1,) * (len(shape) - position - 1))

    loudness = one(*split[0])
    for cut in split[1:]:
        loudness = loudness * one(*cut)
    return loudness


def centred(stream_key, shape, deviation, limit, split=(), held_as=jnp.bfloat16):
    result = deviation * jax.random.normal(stream_key, shape, jnp.float32)
    if split:
        result = result * shard_levels(stream_key, shape, split, -0.22, 0.18)
    return jnp.clip(result, -limit, limit).astype(held_as)


def setup_inputs(seed: int = 0) -> dict:
    seeds = jax.random.split(jax.random.key(seed), 8)
    return {
        "top_grad": centred(seeds[0], (2, TOK, D), 1.0, 6.0, ((2, 64),)),
        "saved_in": centred(seeds[1], (2, SEGMENTS, TOK, D), 1.0, 6.0, ((1, 4), (3, 64))),
        "saved_pre": centred(seeds[2], (2, SEGMENTS, TOK, FF), 1.5, 6.0, ((1, 4), (3, 64))),
        "w_up": draw_w_up(jax.random.fold_in(seeds[7], 71), 0),
        "w_down": draw_w_down(jax.random.fold_in(seeds[7], 71), 0),
        "mask_up": draw_mask_up(jax.random.fold_in(seeds[7], 71), 0),
        "mask_down": draw_mask_down(jax.random.fold_in(seeds[7], 71), 0),
    }


def expand(mask):
    return jnp.repeat(jnp.repeat(mask, BLOCK, axis=0), BLOCK, axis=1).astype(jnp.bfloat16)


def layer_back(grad, x_in, pre, up_w, down_w):
    dh = jnp.dot(grad, down_w.T, preferred_element_type=jnp.float32)
    pre_f = pre.astype(jnp.float32)
    sig = jax.nn.sigmoid(pre_f)
    du = (dh * sig * (1.0 + pre_f * (1.0 - sig))).astype(jnp.bfloat16)
    out = (grad.astype(jnp.float32) + jnp.dot(du, up_w.T, preferred_element_type=jnp.float32)).astype(jnp.bfloat16)
    hidden = jax.nn.silu(pre_f).astype(jnp.bfloat16)
    g_up = jnp.dot(x_in.T, du, preferred_element_type=jnp.float32)
    g_down = jnp.dot(hidden.T, grad, preferred_element_type=jnp.float32)
    return out, g_up, g_down


def reference(top_grad, saved_in, saved_pre, w_up, w_down, mask_up, mask_down):
    grads = [[None] * SEGMENTS for r in range(2)]
    gu = [[None] * SEGMENTS for r in range(2)]
    gd = [[None] * SEGMENTS for r in range(2)]
    for r in range(2):
        grad = top_grad[r]
        for layer in range(SEGMENTS - 1, -1, -1):
            s = layer if r == 0 else SEGMENTS - 1 - layer
            mu = expand(mask_up[r, s])
            md = expand(mask_down[r, s])
            out, g_up, g_down = layer_back(grad, saved_in[r, s], saved_pre[r, s], w_up[r, s] * mu, w_down[r, s] * md)
            grads[r][s] = out
            gu[r][layer] = (g_up * mu.astype(jnp.float32)).astype(jnp.bfloat16)
            gd[r][layer] = (g_down * md.astype(jnp.float32)).astype(jnp.bfloat16)
            grad = out
    half = D // 2
    up_rows = [[None] * SEGMENTS for r in range(2)]
    down_cols = [[None] * SEGMENTS for r in range(2)]
    for layer in range(SEGMENTS):
        su = (gu[0][layer].astype(jnp.float32) + gu[1][layer].astype(jnp.float32)).astype(jnp.bfloat16)
        sd = (gd[0][layer].astype(jnp.float32) + gd[1][layer].astype(jnp.float32)).astype(jnp.bfloat16)
        up_rows[0][layer] = su[:half]
        down_cols[0][layer] = sd[:, :half]
        up_rows[1][SEGMENTS - 1 - layer] = su[half:]
        down_cols[1][SEGMENTS - 1 - layer] = sd[:, half:]
    all_grads = jnp.stack([jnp.stack(grads[r]) for r in range(2)])
    grad_up = jnp.stack([jnp.stack(up_rows[r]) for r in range(2)])
    grad_down = jnp.stack([jnp.stack(down_cols[r]) for r in range(2)])
    return all_grads, grad_up, grad_down
```

```python
import jax
import jax.numpy as jnp
from jax import lax
from jax.sharding import PartitionSpec as P

BLOCK = 128
F32 = jnp.float32
BF16 = jnp.bfloat16


def swap(value, bits):
    return lax.ppermute(value, "segment", [(s, s ^ bits) for s in range(4)])


def exchange(parts):
    return lax.all_to_all(parts, "tp", 0, 0, tiled=True)


def expand(mask):
    return jnp.repeat(jnp.repeat(mask, BLOCK, axis=-2), BLOCK, axis=-1).astype(BF16)


def per_device(top_grad, saved_in, saved_pre, w_up, w_down, mask_up, mask_down):
    members = lax.axis_size("tp")
    section = lax.axis_index("segment")
    place = lax.axis_index("tp")
    core = section & 1
    rep = section >> 1
    outer = (core ^ rep) == 0
    even = core == 0
    features = w_up.shape[2]
    half = features // 2
    share = half // members
    tokens = top_grad.shape[1]

    def pick(condition, a, b):
        return jnp.where(condition, a, b)

    def at(stack, i):
        return lax.dynamic_index_in_dim(stack, i, 0, keepdims=False)

    xs = saved_in[:, 0].transpose(0, 2, 1)
    x_full = lax.all_gather(xs, "tp", axis=1, tiled=True)
    pre = saved_pre[:, 0]
    pre_partner = swap(pre, 3)
    pre_across = swap(at(pre, 1 - rep), 2)
    pre_sibling = swap(at(pre, rep), 1)

    ups_mask = expand(mask_up[:, 0])
    downs_mask = expand(mask_down[:, 0])
    ups = w_up[:, 0] * ups_mask
    downs = w_down[:, 0] * downs_mask

    def up_rows(w, c):
        return lax.dynamic_slice_in_dim(w, c * half, half, 0)

    def up_woven(w, c):
        woven = w.reshape(members, 2, share, w.shape[1])
        return lax.dynamic_index_in_dim(woven, c, 1, keepdims=False).reshape(half, w.shape[1])

    def down_columns(w, c):
        return lax.dynamic_slice_in_dim(w, c * half, half, 1)

    up_first, up_second = at(ups, 1 - rep), at(ups, rep)
    down_first, down_second = at(downs, 1 - rep), at(downs, rep)

    def second_rows(c):
        return pick(outer, up_woven(up_second, c), up_rows(up_second, c))

    keep = [down_columns(down_first, core), up_rows(up_first, core), down_columns(down_second, core), second_rows(core)]
    other = 1 - core
    sent = [down_columns(down_first, other), up_rows(up_first, other), down_columns(down_second, other), second_rows(other)]
    came = [swap(w, 1) for w in sent]
    down_w = {
        3: pick(outer, keep[0], came[0]),
        2: pick(outer, came[0], keep[0]),
        1: pick(outer, came[2], keep[2]),
        0: pick(outer, keep[2], came[2]),
    }
    up_w = {
        3: pick(outer, keep[1], came[1]),
        2: pick(outer, came[1], keep[1]),
        1: pick(outer, came[3], keep[3]),
        0: pick(outer, keep[3], came[3]),
    }
    pre_first, pre_second = at(pre_partner, rep), at(pre, rep)
    pre_of = {
        3: pick(outer, pre_first, pre_across),
        2: pick(outer, pre_across, pre_first),
        1: pick(outer, pre_sibling, pre_second),
        0: pick(outer, pre_second, pre_sibling),
    }

    mine = at(top_grad, rep).T.reshape(2, share, tokens)
    mine = at(mine, core)
    got = exchange(jnp.broadcast_to(mine[None], (members, share, tokens))).reshape(2, members // 2, share, tokens)
    kept = at(got, core)
    traded = swap(at(got, 1 - core), 1)
    grad = pick(even, jnp.stack([kept, traded], 1), jnp.stack([traded, kept], 1)).reshape(half, tokens)

    grads, dus, shards = {}, {}, {}
    for layer in (3, 2, 1, 0):
        grads[layer] = grad
        partial = jnp.dot(down_w[layer], grad, preferred_element_type=F32)
        dh = partial + swap(partial, 1)
        u = pre_of[layer].astype(F32).T
        sig = jax.nn.sigmoid(u)
        du = (dh * sig * (1.0 + u * (1.0 - sig))).astype(BF16)
        dus[layer] = du
        out = jnp.dot(up_w[layer], du, preferred_element_type=F32).astype(BF16)
        landed = exchange(out.reshape(members, share, tokens))
        total = jnp.sum(landed.astype(F32), axis=0)
        if layer:
            own = lax.dynamic_slice_in_dim(grad, place * share, share, 0)
            out = (own.astype(F32) + total).astype(BF16)
            grad = exchange(jnp.broadcast_to(out[None], (members, share, tokens))).reshape(half, tokens)
            mine = lax.dynamic_slice_in_dim(grad, (place % (members // 2)) * 2 * share, 2 * share, 0)
            shards[layer] = pick(place // (members // 2) == core, mine, swap(mine, 1))
        else:
            own = lax.dynamic_slice_in_dim(shards[1], core * share, share, 0)
            out = (own.astype(F32) + total).astype(BF16)
            peer = swap(out, 1)
            shards[0] = pick(even, jnp.concatenate([out, peer]), jnp.concatenate([peer, out]))

    own_out = pick(outer, shards[0], shards[1])
    far_out = swap(pick(outer, shards[2], shards[3]), 2)
    all_grads = pick(rep == 0, jnp.stack([own_out, far_out]), jnp.stack([far_out, own_out]))
    all_grads = all_grads.transpose(0, 2, 1)[:, None]

    x_low = (x_full[0, :half], swap(x_full[1, :half], 3))
    x_high = (swap(x_full[0, half:], 3), x_full[1, half:])

    first_du, second_du = pick(outer, dus[3], dus[2]), pick(outer, dus[0], dus[1])
    far_first, far_second = swap(first_du, 3), swap(second_du, 3)
    near = rep == 0
    low_own, low_far = pick(near, second_du, first_du), pick(near, far_second, far_first)
    high_own, high_far = pick(near, first_du, second_du), pick(near, far_first, far_second)
    du_low = (pick(near, low_own, low_far), pick(near, low_far, low_own))
    du_high = (pick(near, high_own, high_far), pick(near, high_far, high_own))

    hidden = jax.nn.silu(pre.astype(F32)).astype(BF16)
    hidden_far = jax.nn.silu(pre_partner.astype(F32)).astype(BF16)
    h_low = (hidden[0], hidden_far[1])
    h_high = (hidden_far[0], hidden[1])

    g_here = pick(outer, grads[0], grads[2])
    g_across = swap(pick(outer, grads[2], grads[0]), 2)
    g_sibling = swap(pick(outer, grads[1], grads[3]), 1)
    g_partner = swap(pick(outer, grads[3], grads[1]), 3)
    one = (pick(near, g_here, g_across), pick(near, g_across, g_here))
    two = (pick(near, g_sibling, g_partner), pick(near, g_partner, g_sibling))
    g_low = tuple(pick(even, a, b) for a, b in zip(one, two))
    g_high = tuple(pick(even, b, a) for a, b in zip(one, two))

    def up_grad(x, du, mask):
        total = sum(lax.dot_general(a, b, (((1,), (1,)), ((), ())), preferred_element_type=F32) for a, b in zip(x, du))
        return (total * mask.astype(F32)).astype(BF16)

    def down_grad(h, g, mask):
        total = sum(lax.dot_general(a, b, (((0,), (1,)), ((), ())), preferred_element_type=F32) for a, b in zip(h, g))
        return (total * mask.astype(F32)).astype(BF16)

    grad_up = jnp.stack(
        [up_grad(x_low, du_low, ups_mask[0, :half]), up_grad(x_high, du_high, ups_mask[1, half:])]
    )[:, None]
    grad_down = jnp.stack(
        [down_grad(h_low, g_low, downs_mask[0, :, :half]), down_grad(h_high, g_high, downs_mask[1, :, half:])]
    )[:, None]
    return (all_grads, grad_up, grad_down)


def solution(mesh):
    return jax.shard_map(
        per_device,
        mesh=mesh,
        in_specs=(
            P(None, None, "tp"),
            P(None, "segment", None, "tp"),
            P(None, "segment", None, "tp"),
            P(None, "segment", None, "tp"),
            P(None, "segment", "tp", None),
            P(None, "segment", None, "tp"),
            P(None, "segment", "tp", None),
        ),
        out_specs=(
            P(None, "segment", None, "tp"),
            P(None, "segment", None, "tp"),
            P(None, "segment", "tp", None),
        ),
        check_vma=False,
    )
```

```python
import functools

import jax
import jax.numpy as jnp
from jax import lax
from jax.experimental import pallas as pl
from jax.experimental.pallas import tpu as pltpu
from jax.sharding import PartitionSpec as P

BLOCK = 128
F32 = jnp.float32
BF16 = jnp.bfloat16
VMEM_BYTES = 40 << 20
NT = (((1,), (1,)), ((), ()))


def swap(value, bits):
    return lax.ppermute(value, "segment", [(s, s ^ bits) for s in range(4)])


def exchange(parts):
    return lax.all_to_all(parts, "tp", 0, 0, tiled=True)


def pick(condition, a, b):
    return jnp.where(condition, a, b)


def at(stack, i):
    return lax.dynamic_index_in_dim(stack, i, 0, keepdims=False)


def kept_blocks(value, mask):
    return jnp.where(mask > 0, value, jnp.zeros_like(value))


def params():
    return pltpu.CompilerParams(vmem_limit_bytes=VMEM_BYTES)


def prepare_kernel(share, info, mask_u, mask_d, up, down, keep_d, send_d, keep_u, send_u):
    which, core, woven = info[0], info[1], info[2]
    half = keep_u.shape[0]
    blocks = half // BLOCK
    pairs = up.shape[3] // BLOCK

    def columns(b, carry):
        for out, c in ((keep_d, core), (send_d, 1 - core)):
            block = c * blocks + b
            source = pl.ds(pl.multiple_of(block * BLOCK, BLOCK), BLOCK)
            target = pl.ds(pl.multiple_of(b * BLOCK, BLOCK), BLOCK)
            for h in range(pairs):
                rows = slice(h * BLOCK, (h + 1) * BLOCK)
                out[rows, target] = kept_blocks(down[0, 0, rows, source], mask_d[(which * pairs + h) * 2 * blocks + block])
        return carry

    def rows(j, carry):
        for out, c in ((keep_u, core), (send_u, 1 - core)):
            first = jnp.where(woven > 0, (2 * j + c) * share, c * half + j * share)
            source = pl.ds(pl.multiple_of(first, share), share)
            target = pl.ds(pl.multiple_of(j * share, share), share)
            block = first // BLOCK
            for h in range(pairs):
                lanes = slice(h * BLOCK, (h + 1) * BLOCK)
                out[target, lanes] = kept_blocks(up[0, 0, source, lanes], mask_u[(which * 2 * blocks + block) * pairs + h])
        return carry

    lax.fori_loop(0, blocks, columns, 0, unroll=2)
    lax.fori_loop(0, half // share, rows, 0, unroll=4)


def prepare(info, mask_u, mask_d, w_up, w_down, share):
    _, _, features, hidden = w_up.shape
    half = features // 2
    whole = lambda shape: pl.BlockSpec(shape, lambda i, *_: (0, 0))
    return pl.pallas_call(
        functools.partial(prepare_kernel, share),
        grid_spec=pltpu.PrefetchScalarGridSpec(
            num_scalar_prefetch=3,
            grid=(1,),
            in_specs=[
                pl.BlockSpec((1, 1, features, hidden), lambda i, info, *_: (info[0], 0, 0, 0)),
                pl.BlockSpec((1, 1, hidden, features), lambda i, info, *_: (info[0], 0, 0, 0)),
            ],
            out_specs=[whole((hidden, half))] * 2 + [whole((half, hidden))] * 2,
        ),
        out_shape=[jax.ShapeDtypeStruct((hidden, half), BF16)] * 2 + [jax.ShapeDtypeStruct((half, hidden), BF16)] * 2,
        compiler_params=params(),
        cost_estimate=pl.CostEstimate(flops=0, bytes_accessed=8 * features * hidden, transcendentals=0),
        name="prepare",
    )(info, mask_u, mask_d, w_up, w_down)


def fetch(flag, keep, came, held, sem, act):
    for wanted, source in ((1, keep), (0, came)):

        @pl.when(flag[0] == wanted)
        def _(source=source):
            copy = pltpu.make_async_copy(source, held, sem)
            copy.start() if act == "start" else copy.wait()


def down_kernel(flag, keep, came, grad, out, held, sem):
    fetch(flag, keep, came, held, sem, "start")
    fetch(flag, keep, came, held, sem, "wait")
    out[...] = jnp.dot(held[...], grad[...], preferred_element_type=F32)


def down_step(flag, keep, came, grad):
    hidden, half = keep.shape
    tokens = grad.shape[1]
    return pl.pallas_call(
        down_kernel,
        in_specs=[pl.BlockSpec(memory_space=pltpu.SMEM)] + [pl.BlockSpec(memory_space=pl.ANY)] * 2 + [pl.BlockSpec(memory_space=pltpu.VMEM)],
        out_specs=pl.BlockSpec(memory_space=pltpu.VMEM),
        out_shape=jax.ShapeDtypeStruct((hidden, tokens), F32),
        scratch_shapes=[pltpu.VMEM((hidden, half), BF16), pltpu.SemaphoreType.DMA],
        compiler_params=params(),
        cost_estimate=pl.CostEstimate(flops=2 * hidden * half * tokens, bytes_accessed=2 * hidden * half, transcendentals=0),
        name="down",
    )(flag, keep, came, grad)


def up_kernel(flag, keep, came, part, peer, pre, du_out, out, held, sem):
    fetch(flag, keep, came, held, sem, "start")
    u = pre[...].astype(F32)
    sig = jax.nn.sigmoid(u)
    du = ((part[...] + peer[...]) * sig * (1.0 + u * (1.0 - sig))).astype(BF16)
    du_out[...] = du
    fetch(flag, keep, came, held, sem, "wait")
    rows = min(512, out.shape[0])
    for i in range(out.shape[0] // rows):
        at_rows = slice(i * rows, (i + 1) * rows)
        out[at_rows] = jnp.dot(held[at_rows], du, preferred_element_type=F32).astype(BF16)


def up_step(flag, keep, came, part, peer, pre):
    half, hidden = keep.shape
    tokens = part.shape[1]
    vmem = pl.BlockSpec(memory_space=pltpu.VMEM)
    return pl.pallas_call(
        up_kernel,
        in_specs=[pl.BlockSpec(memory_space=pltpu.SMEM)] + [pl.BlockSpec(memory_space=pl.ANY)] * 2 + [vmem] * 3,
        out_specs=[vmem] * 2,
        out_shape=[jax.ShapeDtypeStruct((hidden, tokens), BF16), jax.ShapeDtypeStruct((half, tokens), BF16)],
        scratch_shapes=[pltpu.VMEM((half, hidden), BF16), pltpu.SemaphoreType.DMA],
        compiler_params=params(),
        cost_estimate=pl.CostEstimate(flops=2 * hidden * half * tokens, bytes_accessed=2 * hidden * half, transcendentals=hidden * tokens),
        name="up",
    )(flag, keep, came, part, peer, pre)


def up_grad_kernel(mask_u, x, du, out):
    i = pl.program_id(0)
    rows, hidden = out.shape[2], out.shape[3]
    pairs = hidden // BLOCK
    steps = pl.num_programs(0)
    both = jnp.concatenate([x[0], x[1]], axis=1)
    total = lax.dot_general(both, du[0], NT, preferred_element_type=F32)
    layer = i // (steps // 2)
    blocks = steps * rows // BLOCK
    for b in range(rows // BLOCK):
        at_rows = slice(b * BLOCK, (b + 1) * BLOCK)
        block = i * (rows // BLOCK) + b
        for h in range(pairs):
            lanes = slice(h * BLOCK, (h + 1) * BLOCK)
            out[0, 0, at_rows, lanes] = kept_blocks(total[at_rows, lanes], mask_u[(layer * blocks + block) * pairs + h]).astype(BF16)


def up_grads(mask_u, x, du):
    _, features, tokens = x.shape
    hidden = du.shape[1]
    half = features // 2
    rows = min(512, half)
    per = half // rows
    return pl.pallas_call(
        up_grad_kernel,
        grid_spec=pltpu.PrefetchScalarGridSpec(
            num_scalar_prefetch=1,
            grid=(2 * per,),
            in_specs=[
                pl.BlockSpec((2, rows, tokens), lambda i, _: (0, i, 0)),
                pl.BlockSpec((1, hidden, 2 * tokens), lambda i, _: (i // per, 0, 0)),
            ],
            out_specs=pl.BlockSpec((1, 1, rows, hidden), lambda i, _: (i // per, 0, i % per, 0)),
        ),
        out_shape=jax.ShapeDtypeStruct((2, 1, half, hidden), BF16),
        compiler_params=params(),
        cost_estimate=pl.CostEstimate(flops=4 * features * hidden * tokens, bytes_accessed=4 * features * hidden, transcendentals=0),
        name="up_grads",
    )(mask_u, x, du)


def down_grad_kernel(mask_d, core, h, here, across, sibling, partner, out):
    pair, i = pl.program_id(0), pl.program_id(1)
    hidden, columns = out.shape[2], out.shape[3]
    pairs = hidden // BLOCK
    half_blocks = pl.num_programs(1) * columns // BLOCK
    layer = jnp.where(pair == 0, core[0], 1 - core[0])

    def write(a, b):
        both = jnp.concatenate([a[...], b[...]], axis=1)
        total = lax.dot_general(h[0], both, NT, preferred_element_type=F32)
        for k in range(columns // BLOCK):
            lanes = slice(k * BLOCK, (k + 1) * BLOCK)
            block = layer * half_blocks + i * (columns // BLOCK) + k
            for p in range(pairs):
                rows = slice(p * BLOCK, (p + 1) * BLOCK)
                mask = mask_d[(layer * pairs + p) * 2 * half_blocks + block]
                out[0, 0, rows, lanes] = kept_blocks(total[rows, lanes], mask).astype(BF16)

    @pl.when(pair == 0)
    def _():
        write(here, across)

    @pl.when(pair == 1)
    def _():
        write(sibling, partner)


def down_grads(mask_d, core, h, here, across, sibling, partner):
    half, tokens = here.shape
    hidden = h.shape[1]
    columns = min(512, half)
    per = half // columns
    first = pl.BlockSpec((columns, tokens), lambda p, i, *_: (jnp.where(p == 0, i, per - 1), 0))
    second = pl.BlockSpec((columns, tokens), lambda p, i, *_: (jnp.where(p == 0, 0, i), 0))
    return pl.pallas_call(
        down_grad_kernel,
        grid_spec=pltpu.PrefetchScalarGridSpec(
            num_scalar_prefetch=2,
            grid=(2, per),
            in_specs=[pl.BlockSpec((1, hidden, 2 * tokens), lambda p, i, *_: (p, 0, 0)), first, first, second, second],
            out_specs=pl.BlockSpec(
                (1, 1, hidden, columns), lambda p, i, _, core: (jnp.where(p == 0, core[0], 1 - core[0]), 0, 0, i)
            ),
        ),
        out_shape=jax.ShapeDtypeStruct((2, 1, hidden, half), BF16),
        compiler_params=params(),
        cost_estimate=pl.CostEstimate(flops=8 * half * hidden * tokens, bytes_accessed=8 * half * hidden, transcendentals=0),
        name="down_grads",
    )(mask_d, core, h, here, across, sibling, partner)


def per_device(top_grad, saved_in, saved_pre, w_up, w_down, mask_up, mask_down):
    members = lax.axis_size("tp")
    section = lax.axis_index("segment")
    place = lax.axis_index("tp")
    core = section & 1
    rep = section >> 1
    outer = (core ^ rep) == 0
    even = core == 0
    near = rep == 0
    features = w_up.shape[2]
    half = features // 2
    share = half // members
    tokens = top_grad.shape[1]

    mine = at(at(top_grad, rep).T.reshape(2, share, tokens), core)
    got = exchange(jnp.broadcast_to(mine[None], (members, share, tokens))).reshape(2, members // 2, share, tokens)

    xs = saved_in[:, 0].transpose(0, 2, 1)
    x_far0, x_far1 = swap(xs[0], 3), swap(xs[1], 3)
    low_member = place < members // 2
    x_sent = jnp.stack([pick(low_member, xs[0], x_far0), pick(low_member, x_far1, xs[1])])
    x_full = lax.all_gather(x_sent, "tp", axis=1, tiled=True)

    pre = saved_pre[:, 0].transpose(0, 2, 1)
    pre_partner = swap(pre, 3)
    pre_across = swap(at(pre, 1 - rep), 2)
    pre_sibling = swap(at(pre, rep), 1)

    mask_u, mask_d = mask_up.reshape(-1), mask_down.reshape(-1)
    zero = jnp.zeros((), jnp.int32)
    first_info = jnp.stack([1 - rep, core, zero])
    second_info = jnp.stack([rep, core, outer.astype(jnp.int32)])
    keep_d1, send_d1, keep_u1, send_u1 = prepare(first_info, mask_u, mask_d, w_up, w_down, share)
    came_d1, came_u1 = swap(send_d1, 1), swap(send_u1, 1)
    keep_d2, send_d2, keep_u2, send_u2 = prepare(second_info, mask_u, mask_d, w_up, w_down, share)
    came_d2, came_u2 = swap(send_d2, 1), swap(send_u2, 1)
    at_outer = outer.astype(jnp.int32)[None]
    weights = {
        3: (at_outer, keep_d1, came_d1, keep_u1, came_u1),
        2: (1 - at_outer, keep_d1, came_d1, keep_u1, came_u1),
        1: (1 - at_outer, keep_d2, came_d2, keep_u2, came_u2),
        0: (at_outer, keep_d2, came_d2, keep_u2, came_u2),
    }
    pre_first, pre_second = at(pre_partner, rep), at(pre, rep)
    pre_of = {
        3: pick(outer, pre_first, pre_across),
        2: pick(outer, pre_across, pre_first),
        1: pick(outer, pre_sibling, pre_second),
        0: pick(outer, pre_second, pre_sibling),
    }

    kept = at(got, core)
    traded = swap(at(got, 1 - core), 1)
    grad = pick(even, jnp.stack([kept, traded], 1), jnp.stack([traded, kept], 1)).reshape(half, tokens)

    grads, dus, shards = {}, {}, {}
    for layer in (3, 2, 1, 0):
        grads[layer] = grad
        flag, keep_d, came_d, keep_u, came_u = weights[layer]
        partial = down_step(flag, keep_d, came_d, grad)
        dus[layer], out = up_step(flag, keep_u, came_u, partial, swap(partial, 1), pre_of[layer])
        landed = exchange(out.reshape(members, share, tokens))
        total = jnp.sum(landed.astype(F32), axis=0)
        if layer:
            own = lax.dynamic_slice_in_dim(grad, place * share, share, 0)
            out = (own.astype(F32) + total).astype(BF16)
            grad = exchange(jnp.broadcast_to(out[None], (members, share, tokens))).reshape(half, tokens)
            mine = lax.dynamic_slice_in_dim(grad, (place % (members // 2)) * 2 * share, 2 * share, 0)
            shards[layer] = pick(place // (members // 2) == core, mine, swap(mine, 1))
        else:
            own = lax.dynamic_slice_in_dim(shards[1], core * share, share, 0)
            out = (own.astype(F32) + total).astype(BF16)
            peer = swap(out, 1)
            shards[0] = pick(even, jnp.concatenate([out, peer]), jnp.concatenate([peer, out]))

    own_out = pick(outer, shards[0], shards[1])
    far_out = swap(pick(outer, shards[2], shards[3]), 2)
    all_grads = pick(near, jnp.stack([own_out, far_out]), jnp.stack([far_out, own_out]))
    all_grads = all_grads.transpose(0, 2, 1)[:, None]

    first_du, second_du = pick(outer, dus[3], dus[2]), pick(outer, dus[0], dus[1])
    far_first, far_second = swap(first_du, 3), swap(second_du, 3)
    low_own, low_far = pick(near, second_du, first_du), pick(near, far_second, far_first)
    high_own, high_far = pick(near, first_du, second_du), pick(near, far_first, far_second)
    du_low = jnp.concatenate([pick(near, low_own, low_far), pick(near, low_far, low_own)], 1)
    du_high = jnp.concatenate([pick(near, high_own, high_far), pick(near, high_far, high_own)], 1)
    grad_up = up_grads(mask_u, x_full, jnp.stack([du_low, du_high]))

    hidden = jax.nn.silu(pre.astype(F32)).astype(BF16)
    hidden_far = jax.nn.silu(pre_partner.astype(F32)).astype(BF16)

    def ordered(replica0, replica1):
        return jnp.concatenate([pick(near, replica0, replica1), pick(near, replica1, replica0)], 1)

    h_low, h_high = ordered(hidden[0], hidden_far[1]), ordered(hidden_far[0], hidden[1])
    h_pairs = jnp.stack([pick(even, h_low, h_high), pick(even, h_high, h_low)])
    g_here = pick(outer, grads[0], grads[2])
    g_across = swap(pick(outer, grads[2], grads[0]), 2)
    g_sibling = swap(pick(outer, grads[1], grads[3]), 1)
    g_partner = swap(pick(outer, grads[3], grads[1]), 3)
    grad_down = down_grads(mask_d, core[None], h_pairs, g_here, g_across, g_sibling, g_partner)
    return (all_grads, grad_up, grad_down)


def solution(mesh):
    return jax.shard_map(
        per_device,
        mesh=mesh,
        in_specs=(
            P(None, None, "tp"),
            P(None, "segment", None, "tp"),
            P(None, "segment", None, "tp"),
            P(None, "segment", None, "tp"),
            P(None, "segment", "tp", None),
            P(None, "segment", None, "tp"),
            P(None, "segment", "tp", None),
        ),
        out_specs=(
            P(None, "segment", None, "tp"),
            P(None, "segment", None, "tp"),
            P(None, "segment", "tp", None),
        ),
        check_vma=False,
    )
```

```python
import functools

import jax
import jax.numpy as jnp
from jax import lax
from jax.experimental import pallas as pl
from jax.experimental.pallas import tpu as pltpu
from jax.sharding import PartitionSpec as P

BLOCK = 128
F32 = jnp.float32
BF16 = jnp.bfloat16
VMEM_BYTES = 40 << 20
NT = (((1,), (1,)), ((), ()))


def swap(value, bits):
    return lax.ppermute(value, "segment", [(s, s ^ bits) for s in range(4)])


def exchange(parts):
    return lax.all_to_all(parts, "tp", 0, 0, tiled=True)


def pick(condition, a, b):
    return jnp.where(condition, a, b)


def at(stack, i):
    return lax.dynamic_index_in_dim(stack, i, 0, keepdims=False)


def kept_blocks(value, mask):
    return jnp.where(mask > 0, value, jnp.zeros_like(value))


def params():
    return pltpu.CompilerParams(vmem_limit_bytes=VMEM_BYTES)


def prepare_kernel(share, info, mask_u, mask_d, up, down, keep_d, send_d, keep_u, send_u):
    which, core, woven = info[0], info[1], info[2]
    half = keep_u.shape[0]
    blocks = half // BLOCK
    pairs = up.shape[3] // BLOCK

    def columns(b, carry):
        for out, c in ((keep_d, core), (send_d, 1 - core)):
            block = c * blocks + b
            source = pl.ds(pl.multiple_of(block * BLOCK, BLOCK), BLOCK)
            target = pl.ds(pl.multiple_of(b * BLOCK, BLOCK), BLOCK)
            for h in range(pairs):
                rows = slice(h * BLOCK, (h + 1) * BLOCK)
                out[rows, target] = kept_blocks(down[0, 0, rows, source], mask_d[(which * pairs + h) * 2 * blocks + block])
        return carry

    def rows(j, carry):
        for out, c in ((keep_u, core), (send_u, 1 - core)):
            first = jnp.where(woven > 0, (2 * j + c) * share, c * half + j * share)
            source = pl.ds(pl.multiple_of(first, share), share)
            target = pl.ds(pl.multiple_of(j * share, share), share)
            block = first // BLOCK
            for h in range(pairs):
                lanes = slice(h * BLOCK, (h + 1) * BLOCK)
                out[target, lanes] = kept_blocks(up[0, 0, source, lanes], mask_u[(which * 2 * blocks + block) * pairs + h])
        return carry

    lax.fori_loop(0, blocks, columns, 0, unroll=2)
    lax.fori_loop(0, half // share, rows, 0, unroll=4)


def prepare(info, mask_u, mask_d, w_up, w_down, share):
    _, _, features, hidden = w_up.shape
    half = features // 2
    whole = lambda shape: pl.BlockSpec(shape, lambda i, *_: (0, 0))
    return pl.pallas_call(
        functools.partial(prepare_kernel, share),
        grid_spec=pltpu.PrefetchScalarGridSpec(
            num_scalar_prefetch=3,
            grid=(1,),
            in_specs=[
                pl.BlockSpec((1, 1, features, hidden), lambda i, info, *_: (info[0], 0, 0, 0)),
                pl.BlockSpec((1, 1, hidden, features), lambda i, info, *_: (info[0], 0, 0, 0)),
            ],
            out_specs=[whole((hidden, half))] * 2 + [whole((half, hidden))] * 2,
        ),
        out_shape=[jax.ShapeDtypeStruct((hidden, half), BF16)] * 2 + [jax.ShapeDtypeStruct((half, hidden), BF16)] * 2,
        compiler_params=params(),
        cost_estimate=pl.CostEstimate(flops=0, bytes_accessed=8 * features * hidden, transcendentals=0),
        name="prepare",
    )(info, mask_u, mask_d, w_up, w_down)


def fetch(flag, keep, came, held, sem, act):
    for wanted, source in ((1, keep), (0, came)):

        @pl.when(flag[0] == wanted)
        def _(source=source):
            copy = pltpu.make_async_copy(source, held, sem)
            copy.start() if act == "start" else copy.wait()


def down_kernel(flag, keep, came, grad, out, held, sem):
    fetch(flag, keep, came, held, sem, "start")
    fetch(flag, keep, came, held, sem, "wait")
    out[...] = jnp.dot(held[...], grad[...], preferred_element_type=F32)


def down_step(flag, keep, came, grad):
    hidden, half = keep.shape
    tokens = grad.shape[1]
    return pl.pallas_call(
        down_kernel,
        in_specs=[pl.BlockSpec(memory_space=pltpu.SMEM)] + [pl.BlockSpec(memory_space=pl.ANY)] * 2 + [pl.BlockSpec(memory_space=pltpu.VMEM)],
        out_specs=pl.BlockSpec(memory_space=pltpu.VMEM),
        out_shape=jax.ShapeDtypeStruct((hidden, tokens), F32),
        scratch_shapes=[pltpu.VMEM((hidden, half), BF16), pltpu.SemaphoreType.DMA],
        compiler_params=params(),
        cost_estimate=pl.CostEstimate(flops=2 * hidden * half * tokens, bytes_accessed=2 * hidden * half, transcendentals=0),
        name="down",
    )(flag, keep, came, grad)


def up_kernel(flag, keep, came, part, peer, pre, du_out, out, held, sem):
    fetch(flag, keep, came, held, sem, "start")
    u = pre[...].astype(F32)
    sig = jax.nn.sigmoid(u)
    du = ((part[...] + peer[...]) * sig * (1.0 + u * (1.0 - sig))).astype(BF16)
    du_out[...] = du
    fetch(flag, keep, came, held, sem, "wait")
    rows = min(512, out.shape[0])
    for i in range(out.shape[0] // rows):
        at_rows = slice(i * rows, (i + 1) * rows)
        out[at_rows] = jnp.dot(held[at_rows], du, preferred_element_type=F32).astype(BF16)


def up_step(flag, keep, came, part, peer, pre):
    half, hidden = keep.shape
    tokens = part.shape[1]
    vmem = pl.BlockSpec(memory_space=pltpu.VMEM)
    return pl.pallas_call(
        up_kernel,
        in_specs=[pl.BlockSpec(memory_space=pltpu.SMEM)] + [pl.BlockSpec(memory_space=pl.ANY)] * 2 + [vmem] * 3,
        out_specs=[vmem] * 2,
        out_shape=[jax.ShapeDtypeStruct((hidden, tokens), BF16), jax.ShapeDtypeStruct((half, tokens), BF16)],
        scratch_shapes=[pltpu.VMEM((half, hidden), BF16), pltpu.SemaphoreType.DMA],
        compiler_params=params(),
        cost_estimate=pl.CostEstimate(flops=2 * hidden * half * tokens, bytes_accessed=2 * hidden * half, transcendentals=hidden * tokens),
        name="up",
    )(flag, keep, came, part, peer, pre)


def up_grad_kernel(mask_u, line, x, du, out):
    i = pl.program_id(0)
    rows, hidden = out.shape[2], out.shape[3]
    tokens = x.shape[4]
    pairs = hidden // BLOCK
    steps = pl.num_programs(0)
    both = jnp.concatenate([x[:, 0, 0].reshape(rows, tokens), x[:, 1, 0].reshape(rows, tokens)], axis=1)
    total = lax.dot_general(both, du[0], NT, preferred_element_type=F32)
    layer = i // (steps // 2)
    blocks = steps * rows // BLOCK
    for b in range(rows // BLOCK):
        at_rows = slice(b * BLOCK, (b + 1) * BLOCK)
        block = i * (rows // BLOCK) + b
        for h in range(pairs):
            lanes = slice(h * BLOCK, (h + 1) * BLOCK)
            out[0, 0, at_rows, lanes] = kept_blocks(total[at_rows, lanes], mask_u[(layer * blocks + block) * pairs + h]).astype(BF16)


def up_grads(mask_u, line, x, du):
    inner, _, planes, width, tokens = x.shape
    features = inner * planes * width
    hidden = du.shape[1]
    half = features // 2
    rows = min(512, inner * width)
    per = half // rows
    plane = inner * width // rows
    return pl.pallas_call(
        up_grad_kernel,
        grid_spec=pltpu.PrefetchScalarGridSpec(
            num_scalar_prefetch=2,
            grid=(2 * per,),
            in_specs=[
                pl.BlockSpec(
                    (rows // width, 2, 1, width, tokens), lambda i, _, line: (i % plane, 0, (i // plane) ^ line[0], 0, 0)
                ),
                pl.BlockSpec((1, hidden, 2 * tokens), lambda i, *_: (i // per, 0, 0)),
            ],
            out_specs=pl.BlockSpec((1, 1, rows, hidden), lambda i, *_: (i // per, 0, i % per, 0)),
        ),
        out_shape=jax.ShapeDtypeStruct((2, 1, half, hidden), BF16),
        compiler_params=params(),
        cost_estimate=pl.CostEstimate(flops=4 * features * hidden * tokens, bytes_accessed=4 * features * hidden, transcendentals=0),
        name="up_grads",
    )(mask_u, line, x, du)


def fold_kernel(place, landed, grad, out):
    members, share, _ = landed.shape
    own = grad[pl.ds(pl.multiple_of(place[0] * share, share), share), :].astype(F32)
    total = lax.fori_loop(0, members, lambda j, acc: acc + landed[j].astype(F32), jnp.zeros(own.shape, F32), unroll=8)
    result = (own + total).astype(BF16)

    def put(j, carry):
        out[j] = result
        return carry

    lax.fori_loop(0, members, put, 0, unroll=8)


def fold(place, landed, grad):
    vmem = pl.BlockSpec(memory_space=pltpu.VMEM)
    return pl.pallas_call(
        fold_kernel,
        in_specs=[pl.BlockSpec(memory_space=pltpu.SMEM), vmem, vmem],
        out_specs=vmem,
        out_shape=jax.ShapeDtypeStruct(landed.shape, BF16),
        compiler_params=params(),
        cost_estimate=pl.CostEstimate(flops=landed.size, bytes_accessed=4 * landed.size, transcendentals=0),
        name="fold",
    )(place, landed, grad)


def down_grad_kernel(mask_d, core, h, here, across, sibling, partner, out):
    pair, i = pl.program_id(0), pl.program_id(1)
    hidden, columns = out.shape[2], out.shape[3]
    pairs = hidden // BLOCK
    half_blocks = pl.num_programs(1) * columns // BLOCK
    layer = jnp.where(pair == 0, core[0], 1 - core[0])

    def write(a, b):
        both = jnp.concatenate([a[...], b[...]], axis=1)
        total = lax.dot_general(h[0], both, NT, preferred_element_type=F32)
        for k in range(columns // BLOCK):
            lanes = slice(k * BLOCK, (k + 1) * BLOCK)
            block = layer * half_blocks + i * (columns // BLOCK) + k
            for p in range(pairs):
                rows = slice(p * BLOCK, (p + 1) * BLOCK)
                mask = mask_d[(layer * pairs + p) * 2 * half_blocks + block]
                out[0, 0, rows, lanes] = kept_blocks(total[rows, lanes], mask).astype(BF16)

    @pl.when(pair == 0)
    def _():
        write(here, across)

    @pl.when(pair == 1)
    def _():
        write(sibling, partner)


def down_grads(mask_d, core, h, here, across, sibling, partner):
    half, tokens = here.shape
    hidden = h.shape[1]
    columns = min(512, half)
    per = half // columns
    first = pl.BlockSpec((columns, tokens), lambda p, i, *_: (jnp.where(p == 0, i, per - 1), 0))
    second = pl.BlockSpec((columns, tokens), lambda p, i, *_: (jnp.where(p == 0, 0, i), 0))
    return pl.pallas_call(
        down_grad_kernel,
        grid_spec=pltpu.PrefetchScalarGridSpec(
            num_scalar_prefetch=2,
            grid=(2, per),
            in_specs=[pl.BlockSpec((1, hidden, 2 * tokens), lambda p, i, *_: (p, 0, 0)), first, first, second, second],
            out_specs=pl.BlockSpec(
                (1, 1, hidden, columns), lambda p, i, _, core: (jnp.where(p == 0, core[0], 1 - core[0]), 0, 0, i)
            ),
        ),
        out_shape=jax.ShapeDtypeStruct((2, 1, hidden, half), BF16),
        compiler_params=params(),
        cost_estimate=pl.CostEstimate(flops=8 * half * hidden * tokens, bytes_accessed=8 * half * hidden, transcendentals=0),
        name="down_grads",
    )(mask_d, core, h, here, across, sibling, partner)


def per_device(top_grad, saved_in, saved_pre, w_up, w_down, mask_up, mask_down):
    members = lax.axis_size("tp")
    section = lax.axis_index("segment")
    place = lax.axis_index("tp")
    core = section & 1
    rep = section >> 1
    outer = (core ^ rep) == 0
    even = core == 0
    near = rep == 0
    features = w_up.shape[2]
    half = features // 2
    share = half // members
    tokens = top_grad.shape[1]

    mine = at(at(top_grad, rep).T.reshape(2, share, tokens), core)
    got = exchange(jnp.broadcast_to(mine[None], (members, share, tokens))).reshape(2, members // 2, share, tokens)

    xs = saved_in[:, 0].transpose(0, 2, 1)
    x_far0, x_far1 = swap(xs[0], 3), swap(xs[1], 3)
    low_member = place < members // 2
    x_sent = jnp.stack([pick(low_member, xs[0], x_far0), pick(low_member, x_far1, xs[1])])
    inner = max(1, members // 4)
    planes = members // inner
    lines = [x_sent] + [lax.ppermute(x_sent, "tp", [(i, i ^ (k * inner)) for i in range(members)]) for k in range(1, planes)]
    groups = [[p * inner + q for q in range(inner)] for p in range(planes)]
    x_full = lax.all_gather(jnp.stack(lines, 1), "tp", axis_index_groups=groups)

    pre = saved_pre[:, 0].transpose(0, 2, 1)
    pre_partner = swap(pre, 3)
    pre_across = swap(at(pre, 1 - rep), 2)
    pre_sibling = swap(at(pre, rep), 1)

    mask_u, mask_d = mask_up.reshape(-1), mask_down.reshape(-1)
    zero = jnp.zeros((), jnp.int32)
    first_info = jnp.stack([1 - rep, core, zero])
    second_info = jnp.stack([rep, core, outer.astype(jnp.int32)])
    keep_d1, send_d1, keep_u1, send_u1 = prepare(first_info, mask_u, mask_d, w_up, w_down, share)
    came_d1, came_u1 = swap(send_d1, 1), swap(send_u1, 1)
    keep_d2, send_d2, keep_u2, send_u2 = prepare(second_info, mask_u, mask_d, w_up, w_down, share)
    came_d2, came_u2 = swap(send_d2, 1), swap(send_u2, 1)
    at_outer = outer.astype(jnp.int32)[None]
    weights = {
        3: (at_outer, keep_d1, came_d1, keep_u1, came_u1),
        2: (1 - at_outer, keep_d1, came_d1, keep_u1, came_u1),
        1: (1 - at_outer, keep_d2, came_d2, keep_u2, came_u2),
        0: (at_outer, keep_d2, came_d2, keep_u2, came_u2),
    }
    pre_first, pre_second = at(pre_partner, rep), at(pre, rep)
    pre_of = {
        3: pick(outer, pre_first, pre_across),
        2: pick(outer, pre_across, pre_first),
        1: pick(outer, pre_sibling, pre_second),
        0: pick(outer, pre_second, pre_sibling),
    }

    kept = at(got, core)
    traded = swap(at(got, 1 - core), 1)
    grad = pick(even, jnp.stack([kept, traded], 1), jnp.stack([traded, kept], 1)).reshape(half, tokens)

    grads, dus, shards = {}, {}, {}
    for layer in (3, 2, 1, 0):
        grads[layer] = grad
        flag, keep_d, came_d, keep_u, came_u = weights[layer]
        partial = down_step(flag, keep_d, came_d, grad)
        dus[layer], out = up_step(flag, keep_u, came_u, partial, swap(partial, 1), pre_of[layer])
        landed = exchange(out.reshape(members, share, tokens))
        if layer:
            grad = exchange(fold(place[None], landed, grad)).reshape(half, tokens)
            mine = lax.dynamic_slice_in_dim(grad, (place % (members // 2)) * 2 * share, 2 * share, 0)
            shards[layer] = pick(place // (members // 2) == core, mine, swap(mine, 1))
        else:
            own = lax.dynamic_slice_in_dim(shards[1], core * share, share, 0)
            out = (own.astype(F32) + jnp.sum(landed.astype(F32), axis=0)).astype(BF16)
            peer = swap(out, 1)
            shards[0] = pick(even, jnp.concatenate([out, peer]), jnp.concatenate([peer, out]))

    own_out = pick(outer, shards[0], shards[1])
    far_out = swap(pick(outer, shards[2], shards[3]), 2)
    all_grads = pick(near, jnp.stack([own_out, far_out]), jnp.stack([far_out, own_out]))
    all_grads = all_grads.transpose(0, 2, 1)[:, None]

    first_du, second_du = pick(outer, dus[3], dus[2]), pick(outer, dus[0], dus[1])
    far_first, far_second = swap(first_du, 3), swap(second_du, 3)
    low_own, low_far = pick(near, second_du, first_du), pick(near, far_second, far_first)
    high_own, high_far = pick(near, first_du, second_du), pick(near, far_first, far_second)
    du_low = jnp.concatenate([pick(near, low_own, low_far), pick(near, low_far, low_own)], 1)
    du_high = jnp.concatenate([pick(near, high_own, high_far), pick(near, high_far, high_own)], 1)
    grad_up = up_grads(mask_u, (place // inner)[None], x_full, jnp.stack([du_low, du_high]))

    hidden = jax.nn.silu(pre.astype(F32)).astype(BF16)
    hidden_far = jax.nn.silu(pre_partner.astype(F32)).astype(BF16)

    def ordered(replica0, replica1):
        return jnp.concatenate([pick(near, replica0, replica1), pick(near, replica1, replica0)], 1)

    h_low, h_high = ordered(hidden[0], hidden_far[1]), ordered(hidden_far[0], hidden[1])
    h_pairs = jnp.stack([pick(even, h_low, h_high), pick(even, h_high, h_low)])
    g_here = pick(outer, grads[0], grads[2])
    g_across = swap(pick(outer, grads[2], grads[0]), 2)
    g_sibling = swap(pick(outer, grads[1], grads[3]), 1)
    g_partner = swap(pick(outer, grads[3], grads[1]), 3)
    grad_down = down_grads(mask_d, core[None], h_pairs, g_here, g_across, g_sibling, g_partner)
    return (all_grads, grad_up, grad_down)


def solution(mesh):
    return jax.shard_map(
        per_device,
        mesh=mesh,
        in_specs=(
            P(None, None, "tp"),
            P(None, "segment", None, "tp"),
            P(None, "segment", None, "tp"),
            P(None, "segment", None, "tp"),
            P(None, "segment", "tp", None),
            P(None, "segment", None, "tp"),
            P(None, "segment", "tp", None),
        ),
        out_specs=(
            P(None, "segment", None, "tp"),
            P(None, "segment", None, "tp"),
            P(None, "segment", "tp", None),
        ),
        check_vma=False,
    )
```

```python
import functools

import jax
import jax.numpy as jnp
from jax import lax
from jax.experimental import pallas as pl
from jax.experimental.pallas import tpu as pltpu
from jax.sharding import PartitionSpec as P

BLOCK = 128
F32 = jnp.float32
BF16 = jnp.bfloat16
VMEM_BYTES = 40 << 20
NT = (((1,), (1,)), ((), ()))


def swap(value, bits):
    return lax.ppermute(value, "segment", [(s, s ^ bits) for s in range(4)])


def exchange(parts):
    return lax.all_to_all(parts, "tp", 0, 0, tiled=True)


def pick(condition, a, b):
    return jnp.where(condition, a, b)


def at(stack, i):
    return lax.dynamic_index_in_dim(stack, i, 0, keepdims=False)


def kept_blocks(value, mask):
    return jnp.where(mask > 0, value, jnp.zeros_like(value))


def params():
    return pltpu.CompilerParams(vmem_limit_bytes=VMEM_BYTES)


def prepare_kernel(share, info, mask_u, mask_d, up, down, keep_d, send_d, keep_u, send_u):
    which, core, woven = info[0], info[1], info[2]
    half = keep_u.shape[0]
    blocks = half // BLOCK
    pairs = up.shape[3] // BLOCK

    def columns(b, carry):
        for out, c in ((keep_d, core), (send_d, 1 - core)):
            block = c * blocks + b
            source = pl.ds(pl.multiple_of(block * BLOCK, BLOCK), BLOCK)
            target = pl.ds(pl.multiple_of(b * BLOCK, BLOCK), BLOCK)
            for h in range(pairs):
                rows = slice(h * BLOCK, (h + 1) * BLOCK)
                out[rows, target] = kept_blocks(down[0, 0, rows, source], mask_d[(which * pairs + h) * 2 * blocks + block])
        return carry

    def rows(j, carry):
        for out, c in ((keep_u, core), (send_u, 1 - core)):
            first = jnp.where(woven > 0, (2 * j + c) * share, c * half + j * share)
            source = pl.ds(pl.multiple_of(first, share), share)
            target = pl.ds(pl.multiple_of(j * share, share), share)
            block = first // BLOCK
            for h in range(pairs):
                lanes = slice(h * BLOCK, (h + 1) * BLOCK)
                out[target, lanes] = kept_blocks(up[0, 0, source, lanes], mask_u[(which * 2 * blocks + block) * pairs + h])
        return carry

    lax.fori_loop(0, blocks, columns, 0, unroll=2)
    lax.fori_loop(0, half // share, rows, 0, unroll=4)


def prepare(info, mask_u, mask_d, w_up, w_down, share):
    _, _, features, hidden = w_up.shape
    half = features // 2
    whole = lambda shape: pl.BlockSpec(shape, lambda i, *_: (0, 0))
    return pl.pallas_call(
        functools.partial(prepare_kernel, share),
        grid_spec=pltpu.PrefetchScalarGridSpec(
            num_scalar_prefetch=3,
            grid=(1,),
            in_specs=[
                pl.BlockSpec((1, 1, features, hidden), lambda i, info, *_: (info[0], 0, 0, 0)),
                pl.BlockSpec((1, 1, hidden, features), lambda i, info, *_: (info[0], 0, 0, 0)),
            ],
            out_specs=[whole((hidden, half))] * 2 + [whole((half, hidden))] * 2,
        ),
        out_shape=[jax.ShapeDtypeStruct((hidden, half), BF16)] * 2 + [jax.ShapeDtypeStruct((half, hidden), BF16)] * 2,
        compiler_params=params(),
        cost_estimate=pl.CostEstimate(flops=0, bytes_accessed=8 * features * hidden, transcendentals=0),
        name="prepare",
    )(info, mask_u, mask_d, w_up, w_down)


def fetch(flag, keep, came, held, sem, act):
    for wanted, source in ((1, keep), (0, came)):

        @pl.when(flag[0] == wanted)
        def _(source=source):
            copy = pltpu.make_async_copy(source, held, sem)
            copy.start() if act == "start" else copy.wait()


def down_kernel(flag, keep, came, grad, out, held, sem):
    fetch(flag, keep, came, held, sem, "start")
    fetch(flag, keep, came, held, sem, "wait")
    out[...] = jnp.dot(held[...], grad[...], preferred_element_type=F32)


def down_step(flag, keep, came, grad):
    hidden, half = keep.shape
    tokens = grad.shape[1]
    return pl.pallas_call(
        down_kernel,
        in_specs=[pl.BlockSpec(memory_space=pltpu.SMEM)] + [pl.BlockSpec(memory_space=pl.ANY)] * 2 + [pl.BlockSpec(memory_space=pltpu.VMEM)],
        out_specs=pl.BlockSpec(memory_space=pltpu.VMEM),
        out_shape=jax.ShapeDtypeStruct((hidden, tokens), F32),
        scratch_shapes=[pltpu.VMEM((hidden, half), BF16), pltpu.SemaphoreType.DMA],
        compiler_params=params(),
        cost_estimate=pl.CostEstimate(flops=2 * hidden * half * tokens, bytes_accessed=2 * hidden * half, transcendentals=0),
        name="down",
    )(flag, keep, came, grad)


def up_kernel(flag, keep, came, part, peer, pre, du_out, out, held, sem):
    fetch(flag, keep, came, held, sem, "start")
    u = pre[...].astype(F32)
    sig = jax.nn.sigmoid(u)
    du = ((part[...] + peer[...]) * sig * (1.0 + u * (1.0 - sig))).astype(BF16)
    du_out[...] = du
    fetch(flag, keep, came, held, sem, "wait")
    rows = min(512, out.shape[0])
    for i in range(out.shape[0] // rows):
        at_rows = slice(i * rows, (i + 1) * rows)
        out[at_rows] = jnp.dot(held[at_rows], du, preferred_element_type=F32).astype(BF16)


def up_step(flag, keep, came, part, peer, pre):
    half, hidden = keep.shape
    tokens = part.shape[1]
    vmem = pl.BlockSpec(memory_space=pltpu.VMEM)
    return pl.pallas_call(
        up_kernel,
        in_specs=[pl.BlockSpec(memory_space=pltpu.SMEM)] + [pl.BlockSpec(memory_space=pl.ANY)] * 2 + [vmem] * 3,
        out_specs=[vmem] * 2,
        out_shape=[jax.ShapeDtypeStruct((hidden, tokens), BF16), jax.ShapeDtypeStruct((half, tokens), BF16)],
        scratch_shapes=[pltpu.VMEM((half, hidden), BF16), pltpu.SemaphoreType.DMA],
        compiler_params=params(),
        cost_estimate=pl.CostEstimate(flops=2 * hidden * half * tokens, bytes_accessed=2 * hidden * half, transcendentals=hidden * tokens),
        name="up",
    )(flag, keep, came, part, peer, pre)


def up_grad_kernel(mask_u, line, x, du, out):
    i = pl.program_id(0)
    rows, hidden = out.shape[2], out.shape[3]
    tokens = x.shape[4]
    pairs = hidden // BLOCK
    steps = pl.num_programs(0)
    both = jnp.concatenate([x[:, 0, 0].reshape(rows, tokens), x[:, 1, 0].reshape(rows, tokens)], axis=1)
    total = lax.dot_general(both, du[0], NT, preferred_element_type=F32)
    layer = i // (steps // 2)
    blocks = steps * rows // BLOCK
    for b in range(rows // BLOCK):
        at_rows = slice(b * BLOCK, (b + 1) * BLOCK)
        block = i * (rows // BLOCK) + b
        for h in range(pairs):
            lanes = slice(h * BLOCK, (h + 1) * BLOCK)
            out[0, 0, at_rows, lanes] = kept_blocks(total[at_rows, lanes], mask_u[(layer * blocks + block) * pairs + h]).astype(BF16)


def up_grads(mask_u, line, x, du):
    inner, _, planes, width, tokens = x.shape
    features = inner * planes * width
    hidden = du.shape[1]
    half = features // 2
    rows = min(512, inner * width)
    per = half // rows
    plane = inner * width // rows
    return pl.pallas_call(
        up_grad_kernel,
        grid_spec=pltpu.PrefetchScalarGridSpec(
            num_scalar_prefetch=2,
            grid=(2 * per,),
            in_specs=[
                pl.BlockSpec(
                    (rows // width, 2, 1, width, tokens), lambda i, _, line: (i % plane, 0, (i // plane) ^ line[0], 0, 0)
                ),
                pl.BlockSpec((1, hidden, 2 * tokens), lambda i, *_: (i // per, 0, 0)),
            ],
            out_specs=pl.BlockSpec((1, 1, rows, hidden), lambda i, *_: (i // per, 0, i % per, 0)),
        ),
        out_shape=jax.ShapeDtypeStruct((2, 1, half, hidden), BF16),
        compiler_params=params(),
        cost_estimate=pl.CostEstimate(flops=4 * features * hidden * tokens, bytes_accessed=4 * features * hidden, transcendentals=0),
        name="up_grads",
    )(mask_u, line, x, du)


def fold_kernel(place, landed, grad, out):
    members, share, _ = landed.shape
    own = grad[pl.ds(pl.multiple_of(place[0] * share, share), share), :].astype(F32)
    total = lax.fori_loop(0, members, lambda j, acc: acc + landed[j].astype(F32), jnp.zeros(own.shape, F32), unroll=8)
    result = (own + total).astype(BF16)

    def put(j, carry):
        out[j] = result
        return carry

    lax.fori_loop(0, members, put, 0, unroll=8)


def fold(place, landed, grad):
    vmem = pl.BlockSpec(memory_space=pltpu.VMEM)
    return pl.pallas_call(
        fold_kernel,
        in_specs=[pl.BlockSpec(memory_space=pltpu.SMEM), vmem, vmem],
        out_specs=vmem,
        out_shape=jax.ShapeDtypeStruct(landed.shape, BF16),
        compiler_params=params(),
        cost_estimate=pl.CostEstimate(flops=landed.size, bytes_accessed=4 * landed.size, transcendentals=0),
        name="fold",
    )(place, landed, grad)


def down_grad_kernel(choices, mask_d, info, h, *refs):
    out, grads = refs[-1], refs[: 2 * choices]
    i = pl.program_id(0)
    hidden, columns = out.shape[2], out.shape[3]
    pairs = hidden // BLOCK
    half_blocks = pl.num_programs(0) * columns // BLOCK
    layer = info[0]

    def write(a, b):
        both = jnp.concatenate([a[...], b[...]], axis=1)
        total = lax.dot_general(h[...], both, NT, preferred_element_type=F32)
        for k in range(columns // BLOCK):
            lanes = slice(k * BLOCK, (k + 1) * BLOCK)
            block = layer * half_blocks + i * (columns // BLOCK) + k
            for p in range(pairs):
                rows = slice(p * BLOCK, (p + 1) * BLOCK)
                mask = mask_d[(layer * pairs + p) * 2 * half_blocks + block]
                out[0, 0, rows, lanes] = kept_blocks(total[rows, lanes], mask).astype(BF16)

    for c in range(choices):

        @pl.when(info[1] == c)
        def _(c=c):
            write(grads[2 * c], grads[2 * c + 1])


def down_grads(mask_d, info, h, grads, before=None):
    half, tokens = grads[0][0].shape
    hidden = h.shape[0]
    columns = min(512, half)
    flat = [g for pair in grads for g in pair]
    kept = [] if before is None else [before]
    return pl.pallas_call(
        functools.partial(down_grad_kernel, len(grads)),
        grid_spec=pltpu.PrefetchScalarGridSpec(
            num_scalar_prefetch=2,
            grid=(half // columns,),
            in_specs=[pl.BlockSpec((hidden, 2 * tokens), lambda i, *_: (0, 0))]
            + [pl.BlockSpec((columns, tokens), lambda i, *_: (i, 0))] * len(flat)
            + [pl.BlockSpec(memory_space=pl.ANY)] * len(kept),
            out_specs=pl.BlockSpec((1, 1, hidden, columns), lambda i, _, info: (info[0], 0, 0, i)),
        ),
        out_shape=jax.ShapeDtypeStruct((2, 1, hidden, half), BF16),
        input_output_aliases={3 + len(flat): 0} if kept else {},
        compiler_params=params(),
        cost_estimate=pl.CostEstimate(flops=4 * half * hidden * tokens, bytes_accessed=4 * half * hidden, transcendentals=0),
        name="down_grads",
    )(mask_d, info, h, *flat, *kept)


def per_device(top_grad, saved_in, saved_pre, w_up, w_down, mask_up, mask_down):
    members = lax.axis_size("tp")
    section = lax.axis_index("segment")
    place = lax.axis_index("tp")
    core = section & 1
    rep = section >> 1
    outer = (core ^ rep) == 0
    even = core == 0
    near = rep == 0
    features = w_up.shape[2]
    half = features // 2
    share = half // members
    tokens = top_grad.shape[1]

    mine = at(at(top_grad, rep).T.reshape(2, share, tokens), core)
    got = exchange(jnp.broadcast_to(mine[None], (members, share, tokens))).reshape(2, members // 2, share, tokens)

    xs = saved_in[:, 0].transpose(0, 2, 1)
    x_far0, x_far1 = swap(xs[0], 3), swap(xs[1], 3)
    low_member = place < members // 2
    x_sent = jnp.stack([pick(low_member, xs[0], x_far0), pick(low_member, x_far1, xs[1])])
    inner = max(1, members // 4)
    planes = members // inner
    lines = [x_sent] + [lax.ppermute(x_sent, "tp", [(i, i ^ (k * inner)) for i in range(members)]) for k in range(1, planes)]
    groups = [[p * inner + q for q in range(inner)] for p in range(planes)]
    x_full = lax.all_gather(jnp.stack(lines, 1), "tp", axis_index_groups=groups)

    pre = saved_pre[:, 0].transpose(0, 2, 1)
    pre_partner = swap(pre, 3)
    pre_across = swap(at(pre, 1 - rep), 2)
    pre_sibling = swap(at(pre, rep), 1)

    mask_u, mask_d = mask_up.reshape(-1), mask_down.reshape(-1)
    zero = jnp.zeros((), jnp.int32)
    first_info = jnp.stack([1 - rep, core, zero])
    second_info = jnp.stack([rep, core, outer.astype(jnp.int32)])
    keep_d1, send_d1, keep_u1, send_u1 = prepare(first_info, mask_u, mask_d, w_up, w_down, share)
    came_d1, came_u1 = swap(send_d1, 1), swap(send_u1, 1)
    keep_d2, send_d2, keep_u2, send_u2 = prepare(second_info, mask_u, mask_d, w_up, w_down, share)
    came_d2, came_u2 = swap(send_d2, 1), swap(send_u2, 1)
    at_outer = outer.astype(jnp.int32)[None]
    weights = {
        3: (at_outer, keep_d1, came_d1, keep_u1, came_u1),
        2: (1 - at_outer, keep_d1, came_d1, keep_u1, came_u1),
        1: (1 - at_outer, keep_d2, came_d2, keep_u2, came_u2),
        0: (at_outer, keep_d2, came_d2, keep_u2, came_u2),
    }
    pre_first, pre_second = at(pre_partner, rep), at(pre, rep)
    pre_of = {
        3: pick(outer, pre_first, pre_across),
        2: pick(outer, pre_across, pre_first),
        1: pick(outer, pre_sibling, pre_second),
        0: pick(outer, pre_second, pre_sibling),
    }

    kept = at(got, core)
    traded = swap(at(got, 1 - core), 1)
    grad = pick(even, jnp.stack([kept, traded], 1), jnp.stack([traded, kept], 1)).reshape(half, tokens)

    grads, dus, shards = {}, {}, {}
    for layer in (3, 2, 1, 0):
        grads[layer] = grad
        flag, keep_d, came_d, keep_u, came_u = weights[layer]
        partial = down_step(flag, keep_d, came_d, grad)
        dus[layer], out = up_step(flag, keep_u, came_u, partial, swap(partial, 1), pre_of[layer])
        landed = exchange(out.reshape(members, share, tokens))
        if layer:
            grad = exchange(fold(place[None], landed, grad)).reshape(half, tokens)
            mine = lax.dynamic_slice_in_dim(grad, (place % (members // 2)) * 2 * share, 2 * share, 0)
            shards[layer] = pick(place // (members // 2) == core, mine, swap(mine, 1))
        else:
            own = lax.dynamic_slice_in_dim(shards[1], core * share, share, 0)
            out = (own.astype(F32) + jnp.sum(landed.astype(F32), axis=0)).astype(BF16)
            peer = swap(out, 1)
            shards[0] = pick(even, jnp.concatenate([out, peer]), jnp.concatenate([peer, out]))

    own_out = pick(outer, shards[0], shards[1])
    far_out = swap(pick(outer, shards[2], shards[3]), 2)
    all_grads = pick(near, jnp.stack([own_out, far_out]), jnp.stack([far_out, own_out]))
    all_grads = all_grads.transpose(0, 2, 1)[:, None]

    first_du, second_du = pick(outer, dus[3], dus[2]), pick(outer, dus[0], dus[1])
    far_first, far_second = swap(first_du, 3), swap(second_du, 3)
    far_second, last_grad = lax.optimization_barrier((far_second, grads[0]))
    low_own, low_far = pick(near, second_du, first_du), pick(near, far_second, far_first)
    high_own, high_far = pick(near, first_du, second_du), pick(near, far_first, far_second)
    du_low = jnp.concatenate([pick(near, low_own, low_far), pick(near, low_far, low_own)], 1)
    du_high = jnp.concatenate([pick(near, high_own, high_far), pick(near, high_far, high_own)], 1)
    grad_up = up_grads(mask_u, (place // inner)[None], x_full, jnp.stack([du_low, du_high]))

    hidden = jax.nn.silu(pre.astype(F32)).astype(BF16)
    hidden_far = jax.nn.silu(pre_partner.astype(F32)).astype(BF16)

    def ordered(replica0, replica1):
        return jnp.concatenate([pick(near, replica0, replica1), pick(near, replica1, replica0)], 1)

    h_low, h_high = ordered(hidden[0], hidden_far[1]), ordered(hidden_far[0], hidden[1])
    g_sibling = swap(pick(outer, grads[1], grads[3]), 1)
    g_partner = swap(pick(outer, grads[3], grads[1]), 3)
    grad_down = down_grads(
        mask_d, jnp.stack([1 - core, zero]), pick(even, h_high, h_low), [(g_sibling, g_partner)]
    )
    grad_down = down_grads(
        mask_d,
        jnp.stack([core, outer.astype(jnp.int32)]),
        pick(even, h_low, h_high),
        [(grads[2], swap(grads[2], 2)), (grads[0], swap(last_grad, 2))],
        grad_down,
    )
    return (all_grads, grad_up, grad_down)


def solution(mesh):
    return jax.shard_map(
        per_device,
        mesh=mesh,
        in_specs=(
            P(None, None, "tp"),
            P(None, "segment", None, "tp"),
            P(None, "segment", None, "tp"),
            P(None, "segment", None, "tp"),
            P(None, "segment", "tp", None),
            P(None, "segment", None, "tp"),
            P(None, "segment", "tp", None),
        ),
        out_specs=(
            P(None, "segment", None, "tp"),
            P(None, "segment", None, "tp"),
            P(None, "segment", "tp", None),
        ),
        check_vma=False,
    )
```
